256 devices in a mesh: train: 16 (over z_lo, x, core), feat: 16 (over y, z_hi).
Axes of the slice: x: 4, y: 4, z: 8 (z_hi: 4, z_lo: 2; z = z_hi * 2 + z_lo), core: 2. Of those that a mesh axis runs over, the one named last changes fastest.
Arguments:
- activations: bfloat16 [4096, 4096], P('train', 'feat'), may hold values from -6 to 6
- grad_outputs: bfloat16 [4096, 11008], P('train', 'feat'), may hold values from -6 to 6
- in_basis: bfloat16 [4096, 4096], P('train', 'feat'), may hold values from -0.09375 to 0.09375
- out_basis: bfloat16 [11008, 11008], P('train', 'feat'), may hold values from -0.0546875 to 0.0546875
- eigenvalues: float32 [4096, 11008], P(None, 'feat'), may hold values from 0.2 to 5
- query_left: bfloat16 [4096, 128], P('train'), may hold values from -0.032958984 to 0.032958984
- query_right: bfloat16 [11008, 128], P('train'), may hold values from -0.0017852783 to 0.0017852783
- lengths: int32 [16], P('train'), may hold values from 1 to 256, 2560 in all
Outputs:
- scores: float32 [16, 16], P('train', 'feat')
The draws below stay inside these ranges and needn't reach their ends.
Inputs may be any that keep to these rules, and one draw needn't show every extreme that they name: lengths sum to 2560 and some sequence has 256.
All inputs are finite; a program needn't handle non-finite values. No bound on the sum of `lengths` on one device may be relied on, other than what follows from the above.
Results may differ from the reference program's by a relative error of at most 0.0049.
Values may be sent and summed in bfloat16 or wider, within the bound.
No kernel may reach another device: no remote copies, remote signals or barrier semaphores. Data moves between devices by JAX's collectives and lax.ppermute only.
A program may use at most 128 MiB of HBM per device.

```python
import math
import jax
import jax.numpy as jnp
import numpy as np
from jax import lax

D = 4096
FF = 11008
SEQ_LEN = 256
QUERIES = 16
RANK = 8
SEQS = 16
TOKENS = 4096
QR = 128


def shard_levels(rng, shape, split, smallest, top_value):
    loudness, own = 1.0, jax.random.fold_in(rng, 6)
    for dim, shards_of in split:
        heights = jnp.exp(jax.random.uniform(jax.random.fold_in(own, dim), (shards_of,), jnp.float32, smallest / len(split), top_value / len(split)))
        loudness = loudness * jnp.repeat(heights, shape[dim] // shards_of).reshape([-1 if axis == dim else 1 for axis in range(len(shape))])
    return loudness


def length_profile(count, total, limit, lean):
    portions = [(1 << 20) // math.isqrt(standing ** lean) + 1 for standing in range(2, count + 1)]
    surplus, given = total - limit - (count - 1), [1] * (count - 1)
    while surplus > 0:
        candidates = [i for i in range(count - 1) if given[i] < limit]
        whole, remaining = sum([portions[i] for i in candidates]), surplus
        for i in candidates:
            extra = min(limit - given[i], max(1, remaining * portions[i] // whole), surplus)
            given[i] = given[i] + extra
            surplus = surplus - extra
    return np.array([limit] + given)


def uneven_parts(stream_key, count, total, most, skew):
    if count == 2:
        one = jax.random.randint(stream_key, (), max(1, total - most), min(most, total - 1) + 1)
        return jnp.stack([one, total - one])
    sizes = jnp.asarray(length_profile(count, total, most, skew), jnp.int32)
    twos = (count - 1) // 2
    giver, receiver = sizes[1:1 + 2 * twos:2], sizes[2:2 + 2 * twos:2]
    margin = jnp.minimum(giver - 1, most - receiver)
    moved = jax.random.randint(jax.random.fold_in(stream_key, 1), (twos,), 0, 1 << 20) % (margin + 1)
    sizes = sizes.at[1:1 + 2 * twos:2].set(giver - moved).at[2:2 + 2 * twos:2].set(receiver + moved)
    return sizes[jax.random.permutation(jax.random.fold_in(stream_key, 2), count)]


def gaussian(rng, extent, scale, limit, cuts=(), kind=jnp.bfloat16):
    result = scale * jax.random.normal(rng, extent, jnp.float32)
    if cuts:
        result = result * shard_levels(rng, extent, cuts, -0.22, 0.18)
    return jnp.clip(result, -limit, limit).astype(kind)


def setup_inputs(seed: int = 0) -> dict:
    arg_keys = jax.random.split(jax.random.key(seed), 9)
    return {
        "activations": gaussian(arg_keys[0], (TOKENS, D), 1.0, 6.0, ((0, 16), (1, 16))),
        "grad_outputs": gaussian(arg_keys[1], (TOKENS, FF), 1.0, 6.0, ((0, 16), (1, 16))),
        "in_basis": gaussian(arg_keys[2], (D, D), D ** -0.5, 0.09375, ((0, 16), (1, 16))),
        "out_basis": gaussian(arg_keys[3], (FF, FF), FF ** -0.5, 0.0546875, ((0, 16), (1, 16))),
        "eigenvalues": jnp.clip(jnp.exp(math.log(5.0) - 3.218876 * jax.random.uniform(arg_keys[4], (D, FF), jnp.float32) ** shard_levels(arg_keys[4], (D, FF), ((1, 16),), -0.2, 0.2)), 0.2, 5.0),
        "query_left": gaussian(arg_keys[5], (D, QR), (1.0 / (D * RANK) ** 0.5), 0.032958984, ((0, 16),)),
        "query_right": gaussian(arg_keys[6], (FF, QR), (0.5 / (FF * SEQ_LEN) ** 0.5), 0.0017852783, ((0, 16),)),
        "lengths": uneven_parts(arg_keys[7], SEQS, SEQS * SEQ_LEN * 5 // 8, SEQ_LEN, 2).astype(jnp.int32),
    }


damping = 0.01


def reference(activations, grad_outputs, in_basis, out_basis, eigenvalues, query_left, query_right, lengths):
    contract = (((0,), (0,)), ((), ()))
    in_rot = jnp.dot(activations, in_basis, preferred_element_type=jnp.float32).astype(jnp.bfloat16)
    out_rot = jnp.dot(grad_outputs, out_basis, preferred_element_type=jnp.float32).astype(jnp.bfloat16)
    left_rot = lax.dot_general(in_basis, query_left, contract, preferred_element_type=jnp.float32).astype(jnp.bfloat16)
    right_rot = lax.dot_general(out_basis, query_right, contract, preferred_element_type=jnp.float32).astype(jnp.bfloat16)
    in_seq = in_rot.reshape(SEQS, SEQ_LEN, D)
    out_seq = out_rot.reshape(SEQS, SEQ_LEN, FF)
    positions = jnp.arange(SEQ_LEN, dtype=jnp.int32)
    keep = (positions[None, :] < lengths[:, None].astype(jnp.int32)).astype(jnp.bfloat16)
    out_seq = out_seq * keep[:, :, None]
    divisor = eigenvalues + damping
    left_wide = left_rot.astype(jnp.float32)

    def one_sequence(pair):
        in_rows, out_rows = pair
        grad = lax.dot_general(in_rows, out_rows, contract, preferred_element_type=jnp.float32)
        scaled = (grad / divisor).astype(jnp.bfloat16)
        mapped = jnp.dot(scaled, right_rot, preferred_element_type=jnp.float32)
        return jnp.sum((mapped * left_wide).reshape(D, QUERIES, RANK), axis=(0, 2))

    return lax.map(one_sequence, (in_seq, out_seq))
```

```python
import jax
import jax.numpy as jnp
from jax import lax
from jax.experimental import pallas as pl
from jax.experimental.pallas import tpu as pltpu
from jax.sharding import Mesh, PartitionSpec as P

SEQ_LEN = 256
RANK = 8
damping = 0.01
AXES = ("zlo", "x", "core", "y", "zhi")
SIZES = (2, 4, 2, 4, 4)
TRAIN = ("zlo", "x", "core")
FEAT = ("y", "zhi")
over_rows = (((0,), (0,)), ((), ()))


def shift(block, axis, step):
    size = SIZES[AXES.index(axis)]
    return lax.ppermute(block, axis, [(i, (i + step) % size) for i in range(size)])


def ring(block, axis, cut):
    one, three = shift(block, axis, 1), shift(block, axis, -1)
    two = jnp.concatenate([shift(one[:cut], axis, 1), shift(three[cut:], axis, -1)], axis=0)
    return [block, one, two, three]


def direct(block, axis):
    return [block] + [shift(block, axis, step) for step in (1, 2, 3)]


def rotate_kernel(order, lhs, rhs, out, acc):
    step = pl.program_id(0)

    @pl.when(step == 0)
    def _():
        acc[...] = jnp.zeros_like(acc)

    acc[...] += jnp.dot(lhs[0], rhs[0], preferred_element_type=jnp.float32)

    @pl.when(step == pl.num_programs(0) - 1)
    def _():
        out[...] = acc[...].astype(out.dtype)


def rotate_in(order, lhs, rhs):
    blocks, rows, depth = lhs.shape
    cols = rhs.shape[2]
    return pl.pallas_call(
        rotate_kernel,
        grid_spec=pltpu.PrefetchScalarGridSpec(
            num_scalar_prefetch=1,
            grid=(blocks,),
            in_specs=[
                pl.BlockSpec((1, rows, depth), lambda b, order: (b, 0, 0)),
                pl.BlockSpec((1, depth, cols), lambda b, order: (order[b], 0, 0)),
            ],
            out_specs=pl.BlockSpec((rows, cols), lambda b, order: (0, 0)),
            scratch_shapes=[pltpu.VMEM((rows, cols), jnp.float32)],
        ),
        out_shape=jax.ShapeDtypeStruct((rows, cols), jnp.bfloat16),
        compiler_params=pltpu.CompilerParams(vmem_limit_bytes=32 << 20),
    )(order, lhs, rhs)


def rotate_out_kernel(order, live, lhs, rhs, out, acc):
    step = pl.program_id(0)

    @pl.when(step == 0)
    def _():
        acc[...] = jnp.zeros_like(acc)

    acc[...] += lax.dot_general(lhs[0], rhs[0], over_rows, preferred_element_type=jnp.float32)

    @pl.when(step == pl.num_programs(0) - 1)
    def _():
        position = lax.broadcasted_iota(jnp.int32, acc.shape, 0)
        kept = jnp.where(position < live[0], acc[...], 0.0)
        out[...] = kept.T.astype(out.dtype)


def rotate_out(order, live, lhs, rhs):
    blocks, depth, rows = lhs.shape
    cols = rhs.shape[2]
    return pl.pallas_call(
        rotate_out_kernel,
        grid_spec=pltpu.PrefetchScalarGridSpec(
            num_scalar_prefetch=2,
            grid=(blocks,),
            in_specs=[
                pl.BlockSpec((1, depth, rows), lambda b, order, live: (b, 0, 0)),
                pl.BlockSpec((1, depth, cols), lambda b, order, live: (order[b], 0, 0)),
            ],
            out_specs=pl.BlockSpec((cols, rows), lambda b, order, live: (0, 0)),
            scratch_shapes=[pltpu.VMEM((rows, cols), jnp.float32)],
        ),
        out_shape=jax.ShapeDtypeStruct((cols, rows), jnp.bfloat16),
        compiler_params=pltpu.CompilerParams(vmem_limit_bytes=32 << 20),
    )(order, live, lhs, rhs)


def score_kernel(order, out_t, right, rows, eig, left, total, acc):
    step = pl.program_id(0)

    @pl.when(step == 0)
    def _():
        acc[...] = jnp.zeros_like(acc)

    grad = jnp.dot(out_t[...], rows[0], preferred_element_type=jnp.float32)
    scaled = (grad / (eig[...] + damping)).astype(jnp.bfloat16)
    mapped = jnp.dot(right[...], scaled, preferred_element_type=jnp.float32)
    acc[...] += mapped * left[0].astype(jnp.float32)

    @pl.when(step == pl.num_programs(0) - 1)
    def _():
        total[...] = acc[...]


def score(order, out_t, right, rows, eig_t, left):
    blocks, seq, width = rows.shape
    slab = out_t.shape[0]
    factors = right.shape[0]
    return pl.pallas_call(
        score_kernel,
        grid_spec=pltpu.PrefetchScalarGridSpec(
            num_scalar_prefetch=1,
            grid=(blocks,),
            in_specs=[
                pl.BlockSpec((slab, seq), lambda b, order: (0, 0)),
                pl.BlockSpec((factors, slab), lambda b, order: (0, 0)),
                pl.BlockSpec((1, seq, width), lambda b, order: (b, 0, 0)),
                pl.BlockSpec((slab, width), lambda b, order: (0, order[b])),
                pl.BlockSpec((1, factors, width), lambda b, order: (order[b], 0, 0)),
            ],
            out_specs=pl.BlockSpec((factors, width), lambda b, order: (0, 0)),
            scratch_shapes=[pltpu.VMEM((factors, width), jnp.float32)],
        ),
        out_shape=jax.ShapeDtypeStruct((factors, width), jnp.float32),
        compiler_params=pltpu.CompilerParams(vmem_limit_bytes=32 << 20),
    )(order, out_t, right, rows, eig_t, left)


def local(
    activations, grad_outputs, in_basis, out_basis, eigenvalues, query_left, query_right, lengths
):
    zlo, x, core = lax.axis_index("zlo"), lax.axis_index("x"), lax.axis_index("core")
    y, zhi = lax.axis_index("y"), lax.axis_index("zhi")
    bf16, f32 = jnp.bfloat16, jnp.float32
    trains, feats = 16, 16
    factors = query_left.shape[1]
    slab = out_basis.shape[1]
    width = in_basis.shape[1]

    basis = lax.all_gather(out_basis, TRAIN, axis=0, tiled=False)

    place = jnp.arange(feats, dtype=jnp.int32)
    block_y = lax.rem(y - place // 4 + 4, 4)
    block_z = lax.rem(zhi - place % 4 + 4, 4)
    order = (block_y * 4 + block_z).astype(jnp.int32)

    act_z = jnp.stack(direct(activations, "zhi"))
    act_all = jnp.stack(direct(act_z, "y")).reshape(feats, SEQ_LEN, width)

    u_x = jnp.stack(direct(in_basis, "x"))
    u_z = jnp.stack([u_x, shift(u_x, "zlo", 1)])
    u_all = jnp.stack([u_z, shift(u_z, "core", 1)]).reshape(trains, width, width)
    u_place = (
        lax.rem(core + order, 2) * 8
        + lax.rem(zlo + order // 8, 2) * 4
        + lax.rem(x - lax.rem(order // 2, 4) + 4, 4)
    ).astype(jnp.int32)

    grad_t = jnp.transpose(grad_outputs)
    cut = 352
    grad_z = ring(grad_t, "zhi", cut)
    grad_yz = [ring(block, "y", cut) for block in grad_z]
    grad_all = jnp.stack([grad_yz[z][k] for k in range(4) for z in range(4)])

    left_part = lax.dot_general(query_left, in_basis, over_rows, preferred_element_type=f32)
    right_part = lax.dot_general(query_right, out_basis, over_rows, preferred_element_type=f32)
    share = factors // trains
    parts = jnp.concatenate([right_part, left_part], axis=1).reshape(trains, share, slab + width)
    mine = jnp.sum(lax.all_to_all(parts, TRAIN, 0, 0), axis=0).astype(bf16)
    right_mine, left_mine = mine[:, :slab], mine[:, slab:]
    left_feat = lax.all_to_all(
        jnp.broadcast_to(left_mine[None], (feats, share, width)), FEAT, 0, 0
    )
    left_cols = jnp.transpose(left_feat, (1, 0, 2)).reshape(share, feats * width)
    both = jnp.concatenate([right_mine, left_cols], axis=1)
    both = lax.all_to_all(jnp.broadcast_to(both[None], (trains,) + both.shape), TRAIN, 0, 0)
    both = both.reshape(factors, slab + feats * width)
    right = both[:, :slab]
    left = jnp.transpose(both[:, slab:].reshape(factors, feats, width), (1, 0, 2))

    in_rot = rotate_in(u_place, act_all, u_all)
    in_z = jnp.stack(direct(in_rot, "zhi"))
    in_all = jnp.stack(direct(in_z, "y")).reshape(feats, SEQ_LEN, width)

    out_t = rotate_out(order, lengths, grad_all, basis)
    total = score(order, out_t, right, in_all, jnp.transpose(eigenvalues), left)
    queries = factors // RANK
    partial = jnp.sum(jnp.sum(total, axis=1).reshape(queries, RANK), axis=1)
    pieces = lax.all_to_all(partial.reshape(feats, 1, 1), FEAT, 0, 0)
    return jnp.sum(pieces, axis=0)


def solution(mesh):
    fine = Mesh(mesh.devices.reshape(SIZES), AXES)
    in_specs = (
        P(TRAIN, FEAT),
        P(TRAIN, FEAT),
        P(TRAIN, FEAT),
        P(TRAIN, FEAT),
        P(None, FEAT),
        P(TRAIN, None),
        P(TRAIN, None),
        P(TRAIN),
    )
    return jax.shard_map(
        local, mesh=fine, in_specs=in_specs, out_specs=P(TRAIN, FEAT), check_vma=False
    )
```

```python
import functools

import jax
import jax.numpy as jnp
from jax import lax
from jax.experimental import pallas as pl
from jax.experimental.pallas import tpu as pltpu
from jax.sharding import Mesh, PartitionSpec as P

SEQ_LEN = 256
RANK = 8
damping = 0.01
AXES = ("zlo", "x", "core", "y", "zhi")
SIZES = (2, 4, 2, 4, 4)
TRAIN = ("zlo", "x", "core")
FEAT = ("y", "zhi")
PART = SEQ_LEN // 4
HALF_SCALE = 128.0
over_rows = (((0,), (0,)), ((), ()))


def shift(block, axis, step):
    size = SIZES[AXES.index(axis)]
    return lax.ppermute(block, axis, [(i, (i + step) % size) for i in range(size)])


def ring(block, axis):
    one, three = shift(block, axis, 1), shift(block, axis, -1)
    two = jnp.concatenate([shift(one[:2], axis, 1), shift(three[2:], axis, -1)], axis=0)
    return jnp.stack([block, one, two, three])


def direct(block, axis):
    return jnp.stack([block] + [shift(block, axis, step) for step in (1, 2, 3)])


def to_basis_rows(parts):
    x = lax.axis_index("x")
    got = []
    for k in range(4):
        pairs = []
        for zlo in range(2):
            for sx in range(4):
                for core in range(2):
                    for y in range(4):
                        for zhi in range(4):
                            source = (((zlo * 4 + sx) * 2 + core) * 4 + y) * 4 + zhi
                            dest_x = 2 * (y % 2) + zhi // 2
                            dest = (((y // 2) * 4 + dest_x) * 2 + core) * 4 + (sx + k) % 4
                            pairs.append((source, dest * 4 + 2 * zlo + zhi % 2))
        piece = lax.dynamic_index_in_dim(parts, lax.rem(x + k, 4), 0, keepdims=False)
        got.append(lax.ppermute(piece, AXES, pairs))
    return jnp.stack(got)


def partial_kernel(scale, place, lhs0, lhs1, rhs0, rhs1, out):
    rows = 4 * PART
    depth = lhs0.shape[3]
    result = jnp.dot(lhs0[0].reshape(rows, depth), rhs0[0, 0], preferred_element_type=jnp.float32)
    result += jnp.dot(lhs1[0].reshape(rows, depth), rhs1[0, 0], preferred_element_type=jnp.float32)
    result = (result * scale).astype(out.dtype)
    for k in range(4):
        out[place[4 + k], 0] = result[k * PART : (k + 1) * PART]


def partial_rotation(place, lhs, rhs, out_type, scale):
    depth, cols = rhs.shape[2:]
    return pl.pallas_call(
        functools.partial(partial_kernel, scale),
        grid_spec=pltpu.PrefetchScalarGridSpec(
            num_scalar_prefetch=1,
            grid=(4, 2),
            in_specs=[
                pl.BlockSpec((1, 4, PART, depth), lambda y, z, place: (place[2 * z], 0, 0, 0)),
                pl.BlockSpec((1, 4, PART, depth), lambda y, z, place: (place[2 * z + 1], 0, 0, 0)),
                pl.BlockSpec((1, 1, depth, cols), lambda y, z, place: (0, y, 0, 0)),
                pl.BlockSpec((1, 1, depth, cols), lambda y, z, place: (1, y, 0, 0)),
            ],
            out_specs=pl.BlockSpec((4, 1, PART, cols), lambda y, z, place: (z, y, 0, 0)),
        ),
        out_shape=jax.ShapeDtypeStruct((8, 4, PART, cols), out_type),
        compiler_params=pltpu.CompilerParams(vmem_limit_bytes=40 << 20),
    )(place, lhs, lhs, rhs, rhs)


def score_kernel(place, live, out_ref, right, rows, eig, left, total, acc, out_t):
    step = pl.program_id(0)
    slab = out_ref.shape[2]
    seq, width = 4 * PART, rows.shape[4]

    @pl.when(step == 0)
    def _():
        acc[...] = jnp.zeros_like(acc)
        row = lax.broadcasted_iota(jnp.int32, (PART, slab), 0)
        for k in range(4):
            quarter = place[4 + k]
            kept = jnp.where(row + quarter * PART < live[0], out_ref[quarter].astype(jnp.float32), 0.0)
            out_t[:, k * PART : (k + 1) * PART] = kept.T.astype(out_t.dtype)

    rotated = rows[...].reshape(seq, width)
    grad = jnp.dot(out_t[...], rotated, preferred_element_type=jnp.float32)
    scaled = (grad / (eig[...] + damping)).astype(jnp.bfloat16)
    mapped = jnp.dot(right[...], scaled, preferred_element_type=jnp.float32)
    acc[...] += mapped * left[...].reshape(acc.shape)

    @pl.when(step == pl.num_programs(0) - 1)
    def _():
        total[...] = acc[...]


def score(place, live, out, right, rows, eig_t, left):
    width = rows.shape[4]
    slab = out.shape[2]
    trains, share = left.shape[:2]
    factors = trains * share

    def slab_of(b, place):
        return (b // 4) * 4 + place[8 + b % 4]

    return pl.pallas_call(
        score_kernel,
        grid_spec=pltpu.PrefetchScalarGridSpec(
            num_scalar_prefetch=2,
            grid=(16,),
            in_specs=[
                pl.BlockSpec((4, PART, slab), lambda b, place, live: (0, 0, 0)),
                pl.BlockSpec((factors, slab), lambda b, place, live: (0, 0)),
                pl.BlockSpec((4, 1, 1, PART, width), lambda b, place, live: (0, b % 4, b // 4, 0, 0)),
                pl.BlockSpec((slab, width), lambda b, place, live: (0, slab_of(b, place))),
                pl.BlockSpec((trains, share, width), lambda b, place, live: (0, 0, slab_of(b, place))),
            ],
            out_specs=pl.BlockSpec((factors, width), lambda b, place, live: (0, 0)),
            scratch_shapes=[
                pltpu.VMEM((factors, width), jnp.float32),
                pltpu.VMEM((slab, 4 * PART), jnp.bfloat16),
            ],
        ),
        out_shape=jax.ShapeDtypeStruct((factors, width), jnp.float32),
        compiler_params=pltpu.CompilerParams(vmem_limit_bytes=40 << 20),
    )(place, live, out, right, rows, eig_t, left)


def local(
    activations, grad_outputs, in_basis, out_basis, eigenvalues, query_left, query_right, lengths
):
    y, zhi = lax.axis_index("y"), lax.axis_index("zhi")
    bf16, f32 = jnp.bfloat16, jnp.float32
    trains, feats = 16, 16
    factors = query_left.shape[1]
    slab = out_basis.shape[1]
    width = in_basis.shape[1]

    basis = lax.all_gather(out_basis, ("core", "y"), axis=0, tiled=False).reshape(2, 4, slab, slab)

    four = jnp.arange(4, dtype=jnp.int32)
    step_of_z = lax.rem(zhi - four + 4, 4)
    place = jnp.concatenate([step_of_z, lax.rem(y - four + 4, 4), step_of_z]).astype(jnp.int32)

    u_y = direct(in_basis, "y")
    u_other = shift(u_y, "core", 1)
    core = lax.axis_index("core")
    u_both = jnp.where(core == 0, jnp.stack([u_y, u_other]), jnp.stack([u_other, u_y]))
    u_all = u_both

    act_part = to_basis_rows(activations.reshape(4, PART, width))
    grad_part = to_basis_rows(grad_outputs.reshape(4, PART, slab))
    act_all = direct(act_part, "zhi")
    grad_all = ring(grad_part, "zhi")

    left_part = lax.dot_general(query_left, in_basis, over_rows, preferred_element_type=f32)
    right_part = lax.dot_general(query_right, out_basis, over_rows, preferred_element_type=f32)
    share = factors // trains
    parts = jnp.concatenate([left_part, right_part], axis=1).reshape(trains, share, slab + width)
    mine = jnp.sum(lax.all_to_all(parts, TRAIN, 0, 0), axis=0).astype(bf16)
    left_mine, right_mine = mine[:, :width], mine[:, width:]
    left_feat = lax.all_to_all(
        jnp.broadcast_to(left_mine[None], (feats, share, width)), FEAT, 0, 0
    )
    left_cols = jnp.transpose(left_feat, (1, 0, 2)).reshape(share, feats * width)
    both = jnp.concatenate([left_cols, right_mine], axis=1)
    both = lax.all_to_all(jnp.broadcast_to(both[None], (trains,) + both.shape), TRAIN, 0, 0)
    left = both[:, :, : feats * width].astype(f32)
    right = both[:, :, feats * width :].reshape(factors, slab)

    u_all = jnp.stack([lax.dynamic_index_in_dim(u_all, place[4 + k], 1, keepdims=False) for k in range(4)], axis=1)
    in_part = partial_rotation(place, act_all, u_all, f32, 1.0)
    in_sum = jnp.sum(lax.all_to_all(in_part, ("zlo", "x"), 0, 0, tiled=True), axis=0).astype(bf16)
    in_all = ring(direct(in_sum, "zhi"), "y")

    out_part = partial_rotation(place, grad_all, basis, f32, HALF_SCALE).astype(jnp.float16)
    out_got = lax.all_to_all(out_part, ("zlo", "x"), 0, 0, tiled=True)
    out_sum = (jnp.sum(out_got.astype(f32), axis=0) * (1.0 / HALF_SCALE)).astype(bf16)
    out_rot = lax.all_to_all(out_sum, "y", 0, 0, tiled=True)

    total = score(place, lengths, out_rot, right, in_all, jnp.transpose(eigenvalues), left)
    queries = factors // RANK
    partial = jnp.sum(jnp.sum(total, axis=1).reshape(queries, RANK), axis=1)
    pieces = lax.all_to_all(partial.reshape(feats, 1, 1), FEAT, 0, 0)
    return jnp.sum(pieces, axis=0)


def solution(mesh):
    fine = Mesh(mesh.devices.reshape(SIZES), AXES)
    in_specs = (
        P(TRAIN, FEAT),
        P(TRAIN, FEAT),
        P(TRAIN, FEAT),
        P(TRAIN, FEAT),
        P(None, FEAT),
        P(TRAIN, None),
        P(TRAIN, None),
        P(TRAIN),
    )
    return jax.shard_map(
        local, mesh=fine, in_specs=in_specs, out_specs=P(TRAIN, FEAT), check_vma=False
    )
```

```python
import functools

import jax
import jax.numpy as jnp
from jax import lax
from jax.experimental import pallas as pl
from jax.experimental.pallas import tpu as pltpu
from jax.sharding import Mesh, PartitionSpec as P

SEQ_LEN = 256
RANK = 8
VMEM_LIMIT = 16 << 20
SCORE_LIMIT = 54 << 20
GROUPS = ((0,), (1, 3), (2,))
PIECES = 15
damping = 0.01
AXES = ("zlo", "x", "core", "y", "zhi")
SIZES = (2, 4, 2, 4, 4)
TRAIN = ("zlo", "x", "core")
FEAT = ("y", "zhi")
over_rows = (((0,), (0,)), ((), ()))


def shift(block, axis, step):
    size = SIZES[AXES.index(axis)]
    return lax.ppermute(block, axis, [(i, (i + step) % size) for i in range(size)])


def sides(block, axis):
    return shift(block, axis, 1), shift(block, axis, -1)


def opposite(one, three, axis):
    cut = one.shape[-2] // 2
    return shift(one[..., :cut, :], axis, 1), shift(three[..., cut:, :], axis, -1)


def direct(block, axis):
    return [block] + [shift(block, axis, step) for step in (1, 2, 3)]


def after(value, *earlier):
    return lax.optimization_barrier((value, *earlier))[0]


def everyone(block, axes, size):
    return lax.all_to_all(jnp.broadcast_to(block[None], (size,) + block.shape), axes, 0, 0)


def rotate_in_kernel(order, lhs, rhs, out, acc, acc_left):
    step = pl.program_id(0)
    width = lhs.shape[2]
    half = acc_left.shape[0]

    @pl.when(step == 0)
    def _():
        acc[...] = jnp.zeros_like(acc)
        acc_left[...] = jnp.zeros_like(acc_left)

    basis = rhs[0, :, :width]
    acc[...] += jnp.dot(lhs[0], basis, preferred_element_type=jnp.float32)
    acc_left[...] += lax.dot_general(
        rhs[0, :, width:], basis, over_rows, preferred_element_type=jnp.float32
    )

    @pl.when(step == pl.num_programs(0) - 1)
    def _():
        rows = acc.shape[0]
        out[:rows] = acc[...].astype(out.dtype)
        core = order[pl.num_programs(0)]
        mine = jnp.where(core == 0, acc_left[:half // 2], acc_left[half // 2 :])
        out[rows:] = mine.astype(out.dtype)


def rotate_in(order, lhs, rhs):
    blocks, rows, depth = lhs.shape
    cols = depth
    factors = rhs.shape[2] - cols
    return pl.pallas_call(
        rotate_in_kernel,
        grid_spec=pltpu.PrefetchScalarGridSpec(
            num_scalar_prefetch=1,
            grid=(blocks,),
            in_specs=[
                pl.BlockSpec((1, rows, depth), lambda b, order: (b, 0, 0)),
                pl.BlockSpec((1, depth, cols + factors), lambda b, order: (order[b], 0, 0)),
            ],
            out_specs=pl.BlockSpec((rows + factors // 2, cols), lambda b, order: (0, 0)),
            scratch_shapes=[
                pltpu.VMEM((rows, cols), jnp.float32),
                pltpu.VMEM((factors, cols), jnp.float32),
            ],
        ),
        out_shape=jax.ShapeDtypeStruct((rows + factors // 2, cols), jnp.bfloat16),
        compiler_params=pltpu.CompilerParams(vmem_limit_bytes=VMEM_LIMIT),
    )(order, lhs, rhs)


def score_kernel(order, columns, live, *refs):
    lhs, rest = refs[:PIECES], refs[PIECES:]
    right, rows, left, eig_hbm, near, far, out, met, acc, eig, held, lhs_sems, eig_sems, sems = rest
    slots = held.shape[0]
    ahead, width = eig.shape[0], eig.shape[2]

    def bring(number):
        start = pl.multiple_of(columns[number] * width, width)
        return pltpu.make_async_copy(
            eig_hbm.at[:, pl.ds(start, width)], eig.at[number % ahead], eig_sems.at[number % ahead]
        )

    for number in range(ahead - 1):
        bring(number).start()
    half = near.shape[0]
    moves, first = [], 0
    for base, count in ((0, 1), (5, 2), (10, 1)):
        cut = lhs[base + 2].shape[1]
        for piece, row in ((base, 0), (base + 1, 0), (base + 4, 0), (base + 2, 0), (base + 3, cut)):
            target = met.at[pl.ds(first, count), pl.ds(row, lhs[piece].shape[1])]
            moves.append((first, pltpu.make_async_copy(lhs[piece], target, lhs_sems.at[piece])))
            if piece != base + 2:
                first += count
    for _, move in moves:
        move.start()

    def fetch(number, act):
        slot = number % slots

        @pl.when(order[number] < half)
        def _():
            act(pltpu.make_async_copy(near.at[jnp.minimum(order[number], half - 1)], held.at[slot], sems.at[slot]))

        @pl.when(order[number] >= half)
        def _():
            act(pltpu.make_async_copy(far.at[jnp.maximum(order[number] - half, 0)], held.at[slot], sems.at[slot]))

    for number in range(slots - 1):
        fetch(number, lambda copy: copy.start())
    depth = near.shape[1]
    for number in range(met.shape[0]):
        if number + slots - 1 < met.shape[0]:
            fetch(number + slots - 1, lambda copy: copy.start())
        fetch(number, lambda copy: copy.wait())
        for first, move in moves:
            if first == number:
                move.wait()
        term = jnp.dot(
            met[number, :, :depth], held[number % slots], preferred_element_type=jnp.float32
        )
        if number == 0:
            acc[...] = term
        else:
            acc[...] += term
    position = lax.broadcasted_iota(jnp.int32, acc.shape, 0)
    out_t = jnp.where(position < live[0], acc[...], 0.0).astype(jnp.bfloat16).T
    seq = acc.shape[0]
    total = jnp.zeros(out.shape, jnp.float32)
    for i in range(rows.shape[0]):
        if i + ahead - 1 < rows.shape[0]:
            bring(i + ahead - 1).start()
        grad = jnp.dot(out_t, rows[i, :seq], preferred_element_type=jnp.float32)
        bring(i).wait()
        scaled = (grad / (eig[i % ahead] + damping)).astype(jnp.bfloat16)
        mapped = jnp.dot(right[...], scaled, preferred_element_type=jnp.float32)
        factors = jnp.concatenate([rows[i, seq:], left[i]], axis=0)
        total += mapped * factors.astype(jnp.float32)
    out[...] = total


def score(order, columns, live, lhs, near, far, right, rows, eig_t, left):
    (height, padded), cols = lhs[0].shape[1:], near.shape[2]
    factors, width = right.shape[0], rows.shape[2]
    vmem, smem = pl.BlockSpec(memory_space=pltpu.VMEM), pl.BlockSpec(memory_space=pltpu.SMEM)
    hbm = pl.BlockSpec(memory_space=pltpu.HBM)
    return pl.pallas_call(
        score_kernel,
        in_specs=[smem] * 3 + [hbm] * PIECES + [vmem] * 3 + [hbm] * 3,
        out_specs=vmem,
        scratch_shapes=[
            pltpu.VMEM((16, height, padded), jnp.bfloat16),
            pltpu.VMEM((height, cols), jnp.float32),
            pltpu.VMEM((4, cols, width), jnp.float32),
            pltpu.VMEM((4,) + near.shape[1:], jnp.bfloat16),
            pltpu.SemaphoreType.DMA((PIECES,)),
            pltpu.SemaphoreType.DMA((4,)),
            pltpu.SemaphoreType.DMA((4,)),
        ],
        out_shape=jax.ShapeDtypeStruct((factors, width), jnp.float32),
        compiler_params=pltpu.CompilerParams(vmem_limit_bytes=SCORE_LIMIT),
    )(order, columns, live, *lhs, right, rows, left, eig_t, near, far)


def local(
    activations, grad_outputs, in_basis, out_basis, eigenvalues, query_left, query_right, lengths
):
    zlo, x, core = lax.axis_index("zlo"), lax.axis_index("x"), lax.axis_index("core")
    y, zhi = lax.axis_index("y"), lax.axis_index("zhi")
    bf16, f32 = jnp.bfloat16, jnp.float32
    trains, feats = 16, 16
    factors = query_left.shape[1]
    share = factors // trains
    slab = out_basis.shape[1]
    width = in_basis.shape[1]

    u_own = jnp.concatenate([in_basis, query_left], axis=1)
    u_far = shift(u_own, "zlo", 1)
    u_all = lax.all_gather(jnp.stack([u_own, u_far]), ("x", "core"), axis=0, tiled=True)
    near = lax.all_gather(after(out_basis, u_far), ("x", "core"), axis=0, tiled=False)
    block = jnp.arange(feats, dtype=jnp.int32)
    u_place = lax.rem(block, 8) * 2 + lax.rem(zlo + block // 8, 2)

    right_part = lax.dot_general(query_right, out_basis, over_rows, preferred_element_type=f32)
    half = factors // 2
    low, high = right_part[:half], right_part[half:]
    right_core = jnp.where(core == 0, low, high) + shift(jnp.where(core == 0, high, low), "core", 1)
    right_pair = right_core + shift(right_core, "zlo", 1)
    right_x = right_pair + lax.ppermute(right_pair, "x", [(i, i ^ 1) for i in range(4)])
    right_sum = right_x + lax.ppermute(right_x, "x", [(i, i ^ 2) for i in range(4)])
    right_own = right_sum.astype(bf16)

    act_z = everyone(after(activations, u_far), "zhi", 4)
    padding = -slab % 256
    own = jnp.pad(grad_outputs, ((0, 0), (0, padding)))[None]
    own_1, own_3 = sides(own, "y")

    act_all = everyone(after(act_z, own_1, own_3, right_core), "y", 4).reshape(feats, SEQ_LEN, width)
    z_1, z_3 = sides(after(own, act_z), "zhi")
    own_2 = opposite(own_1, own_3, "y")
    in_rot = rotate_in(
        jnp.concatenate([u_place, core[None].astype(jnp.int32)]),
        after(act_all, z_1, z_3, *own_2, right_pair),
        u_all,
    )

    pair = jnp.concatenate([z_1, z_3], axis=0)
    pair_1, pair_3 = sides(pair, "y")
    v_far = shift(after(out_basis, z_1, z_3), "zlo", 1)
    in_z = everyone(after(in_rot, right_x), "zhi", 4)
    z_2 = jnp.concatenate(opposite(after(z_1, right_own), after(z_3, right_own), "zhi"), axis=-2)
    far = lax.all_gather(after(v_far, in_z, pair_1, pair_3), ("x", "core"), axis=0, tiled=False)

    in_all = everyone(after(in_z, pair_1, pair_3), "y", 4)
    in_all = in_all.reshape(feats, SEQ_LEN + factors // 2, width)
    pair_2 = opposite(pair_1, pair_3, "y")
    far_1, far_3 = sides(z_2, "y")
    far_2 = opposite(far_1, far_3, "y")

    left_other = shift(in_all[:, SEQ_LEN:], "core", 1)

    pieces = (own, own_1, *own_2, own_3, pair, pair_1, *pair_2, pair_3, z_2, far_1, *far_2, far_3)
    steps = [(k, z) for group in GROUPS for k in (0, 1, 3, 2) for z in group]
    y_steps, z_steps = (jnp.array(v, jnp.int32) for v in zip(*steps))
    numbers = lax.rem(y - y_steps + 4, 4) * 4 + lax.rem(zhi - z_steps + 4, 4)
    numbers = lax.rem(numbers - zlo * 8 + 16, 16).astype(jnp.int32)

    right_here = jnp.concatenate([right_own, shift(right_own, "core", 1)], axis=0)
    eig_t = jnp.transpose(eigenvalues)
    total = score(
        numbers, block, lengths, pieces, near, far, right_here, in_all, eig_t, left_other
    )
    sums = jnp.sum(total, axis=1)
    sums = jnp.where(core == 0, sums, jnp.concatenate([sums[half:], sums[:half]]))
    queries = factors // RANK
    partial = jnp.sum(sums.reshape(queries, RANK), axis=1)
    pieces = lax.all_to_all(partial.reshape(feats, 1, 1), FEAT, 0, 0)
    return jnp.sum(pieces, axis=0)


def solution(mesh):
    fine = Mesh(mesh.devices.reshape(SIZES), AXES)
    in_specs = (
        P(TRAIN, FEAT),
        P(TRAIN, FEAT),
        P(TRAIN, FEAT),
        P(TRAIN, FEAT),
        P(None, FEAT),
        P(TRAIN, None),
        P(TRAIN, None),
        P(TRAIN),
    )
    return jax.shard_map(
        local, mesh=fine, in_specs=in_specs, out_specs=P(TRAIN, FEAT), check_vma=False
    )
```

```python
import functools

import jax
import jax.numpy as jnp
from jax import lax
from jax.experimental import pallas as pl
from jax.experimental.pallas import tpu as pltpu
from jax.sharding import Mesh, PartitionSpec as P

SEQ_LEN = 256
RANK = 8
VMEM_LIMIT = 16 << 20
SCORE_LIMIT = 54 << 20
GROUPS = ((0,), (1, 3), (2,))
PIECES = 20
damping = 0.01
AXES = ("zlo", "x", "core", "y", "zhi")
SIZES = (2, 4, 2, 4, 4)
TRAIN = ("zlo", "x", "core")
FEAT = ("y", "zhi")
over_rows = (((0,), (0,)), ((), ()))


def shift(block, axis, step):
    size = SIZES[AXES.index(axis)]
    return lax.ppermute(block, axis, [(i, (i + step) % size) for i in range(size)])


def sides(block, axis):
    return shift(block, axis, 1), shift(block, axis, -1)


def opposite(one, three, axis):
    cut = one.shape[-2] // 2
    return shift(one[..., :cut, :], axis, 1), shift(three[..., cut:, :], axis, -1)


def direct(block, axis):
    return [block] + [shift(block, axis, step) for step in (1, 2, 3)]


def after(value, *earlier):
    return lax.optimization_barrier((value, *earlier))[0]


def everyone(block, axes, size):
    return lax.all_to_all(jnp.broadcast_to(block[None], (size,) + block.shape), axes, 0, 0)


def rotate_in_kernel(order, lhs, rhs, out, acc, acc_left):
    step = pl.program_id(0)
    width = lhs.shape[2]
    half = acc_left.shape[0]

    @pl.when(step == 0)
    def _():
        acc[...] = jnp.zeros_like(acc)
        acc_left[...] = jnp.zeros_like(acc_left)

    basis = rhs[0, :, :width]
    acc[...] += jnp.dot(lhs[0], basis, preferred_element_type=jnp.float32)
    acc_left[...] += lax.dot_general(
        rhs[0, :, width:], basis, over_rows, preferred_element_type=jnp.float32
    )

    @pl.when(step == pl.num_programs(0) - 1)
    def _():
        rows = acc.shape[0]
        out[:rows] = acc[...].astype(out.dtype)
        core = order[pl.num_programs(0)]
        mine = jnp.where(core == 0, acc_left[:half // 2], acc_left[half // 2 :])
        out[rows:] = mine.astype(out.dtype)


def rotate_in(order, lhs, rhs):
    blocks, rows, depth = lhs.shape
    cols = depth
    factors = rhs.shape[2] - cols
    return pl.pallas_call(
        rotate_in_kernel,
        grid_spec=pltpu.PrefetchScalarGridSpec(
            num_scalar_prefetch=1,
            grid=(blocks,),
            in_specs=[
                pl.BlockSpec((1, rows, depth), lambda b, order: (b, 0, 0)),
                pl.BlockSpec((1, depth, cols + factors), lambda b, order: (order[b], 0, 0)),
            ],
            out_specs=pl.BlockSpec((rows + factors // 2, cols), lambda b, order: (0, 0)),
            scratch_shapes=[
                pltpu.VMEM((rows, cols), jnp.float32),
                pltpu.VMEM((factors, cols), jnp.float32),
            ],
        ),
        out_shape=jax.ShapeDtypeStruct((rows + factors // 2, cols), jnp.bfloat16),
        compiler_params=pltpu.CompilerParams(vmem_limit_bytes=VMEM_LIMIT),
    )(order, lhs, rhs)


def score_kernel(order, columns, live, *refs):
    lhs, rest = refs[:PIECES], refs[PIECES:]
    right, left, eig_hbm, near, far, out, met, rows, acc, eig, held, lhs_sems, eig_sems, sems = rest
    slots = held.shape[0]
    ahead, width = eig.shape[0], eig.shape[2]

    def bring(number):
        start = pl.multiple_of(columns[number] * width, width)
        return pltpu.make_async_copy(
            eig_hbm.at[:, pl.ds(start, width)], eig.at[number % ahead], eig_sems.at[number % ahead]
        )

    for number in range(ahead - 1):
        bring(number).start()
    half = near.shape[0]
    moves = {}
    for held_in, bases in ((met, ((0, 1), (5, 2), (10, 1))), (rows, ((15, 4),))):
        first = 0
        for base, count in bases:
            cut = lhs[base + 2].shape[1]
            for piece, row in ((base, 0), (base + 1, 0), (base + 4, 0), (base + 2, 0), (base + 3, cut)):
                target = held_in.at[pl.ds(first, count), pl.ds(row, lhs[piece].shape[1])]
                move = pltpu.make_async_copy(lhs[piece], target, lhs_sems.at[piece])
                moves.setdefault((held_in is met, first), []).append(move)
                move.start()
                if piece != base + 2:
                    first += count

    def fetch(number, act):
        slot = number % slots

        @pl.when(order[number] < half)
        def _():
            act(pltpu.make_async_copy(near.at[jnp.minimum(order[number], half - 1)], held.at[slot], sems.at[slot]))

        @pl.when(order[number] >= half)
        def _():
            act(pltpu.make_async_copy(far.at[jnp.maximum(order[number] - half, 0)], held.at[slot], sems.at[slot]))

    for number in range(slots - 1):
        fetch(number, lambda copy: copy.start())
    depth = near.shape[1]
    for number in range(met.shape[0]):
        if number + slots - 1 < met.shape[0]:
            fetch(number + slots - 1, lambda copy: copy.start())
        fetch(number, lambda copy: copy.wait())
        for move in moves.get((True, number), ()):
            move.wait()
        term = jnp.dot(
            met[number, :, :depth], held[number % slots], preferred_element_type=jnp.float32
        )
        if number == 0:
            acc[...] = term
        else:
            acc[...] += term
    position = lax.broadcasted_iota(jnp.int32, acc.shape, 0)
    out_t = jnp.where(position < live[0], acc[...], 0.0).astype(jnp.bfloat16).T
    seq = acc.shape[0]
    total = jnp.zeros(out.shape, jnp.float32)
    for i in range(rows.shape[0]):
        if i + ahead - 1 < rows.shape[0]:
            bring(i + ahead - 1).start()
        for move in moves.get((False, i), ()):
            move.wait()
        grad = jnp.dot(out_t, rows[i, :seq], preferred_element_type=jnp.float32)
        bring(i).wait()
        scaled = (grad / (eig[i % ahead] + damping)).astype(jnp.bfloat16)
        mapped = jnp.dot(right[...], scaled, preferred_element_type=jnp.float32)
        factors = jnp.concatenate([rows[i, seq:], left[i]], axis=0)
        total += mapped * factors.astype(jnp.float32)
    out[...] = total


def score(order, columns, live, lhs, rows, near, far, right, eig_t, left):
    (height, padded), cols = lhs[0].shape[1:], near.shape[2]
    factors, width = right.shape[0], rows[0].shape[2]
    vmem, smem = pl.BlockSpec(memory_space=pltpu.VMEM), pl.BlockSpec(memory_space=pltpu.SMEM)
    hbm = pl.BlockSpec(memory_space=pltpu.HBM)
    return pl.pallas_call(
        score_kernel,
        in_specs=[smem] * 3 + [hbm] * PIECES + [vmem] * 2 + [hbm] * 3,
        out_specs=vmem,
        scratch_shapes=[
            pltpu.VMEM((16, height, padded), jnp.bfloat16),
            pltpu.VMEM((16,) + rows[0].shape[1:], jnp.bfloat16),
            pltpu.VMEM((height, cols), jnp.float32),
            pltpu.VMEM((4, cols, width), jnp.float32),
            pltpu.VMEM((4,) + near.shape[1:], jnp.bfloat16),
            pltpu.SemaphoreType.DMA((PIECES,)),
            pltpu.SemaphoreType.DMA((4,)),
            pltpu.SemaphoreType.DMA((4,)),
        ],
        out_shape=jax.ShapeDtypeStruct((factors, width), jnp.float32),
        compiler_params=pltpu.CompilerParams(vmem_limit_bytes=SCORE_LIMIT),
    )(order, columns, live, *lhs, *rows, right, left, eig_t, near, far)


def local(
    activations, grad_outputs, in_basis, out_basis, eigenvalues, query_left, query_right, lengths
):
    zlo, x, core = lax.axis_index("zlo"), lax.axis_index("x"), lax.axis_index("core")
    y, zhi = lax.axis_index("y"), lax.axis_index("zhi")
    bf16, f32 = jnp.bfloat16, jnp.float32
    trains, feats = 16, 16
    factors = query_left.shape[1]
    share = factors // trains
    slab = out_basis.shape[1]
    width = in_basis.shape[1]

    u_own = jnp.concatenate([in_basis, query_left], axis=1)
    u_far = shift(u_own, "zlo", 1)
    u_all = lax.all_gather(jnp.stack([u_own, u_far]), ("x", "core"), axis=0, tiled=True)
    near = lax.all_gather(after(out_basis, u_far), ("x", "core"), axis=0, tiled=False)
    block = jnp.arange(feats, dtype=jnp.int32)
    u_place = lax.rem(block, 8) * 2 + lax.rem(zlo + block // 8, 2)

    right_part = lax.dot_general(query_right, out_basis, over_rows, preferred_element_type=f32)
    half = factors // 2
    low, high = right_part[:half], right_part[half:]
    right_core = jnp.where(core == 0, low, high) + shift(jnp.where(core == 0, high, low), "core", 1)
    right_pair = right_core + shift(right_core, "zlo", 1)
    right_x = right_pair + lax.ppermute(right_pair, "x", [(i, i ^ 1) for i in range(4)])
    right_sum = right_x + lax.ppermute(right_x, "x", [(i, i ^ 2) for i in range(4)])
    right_own = right_sum.astype(bf16)

    act_z = everyone(after(activations, u_far), "zhi", 4)
    padding = -slab % 256
    own = jnp.pad(grad_outputs, ((0, 0), (0, padding)))[None]
    own_1, own_3 = sides(own, "y")

    act_all = everyone(after(act_z, own_1, own_3, right_core), "y", 4).reshape(feats, SEQ_LEN, width)
    z_1, z_3 = sides(after(own, act_z), "zhi")
    own_2 = opposite(own_1, own_3, "y")
    in_rot = rotate_in(
        jnp.concatenate([u_place, core[None].astype(jnp.int32)]),
        after(act_all, z_1, z_3, *own_2, right_pair),
        u_all,
    )

    pair = jnp.concatenate([z_1, z_3], axis=0)
    pair_1, pair_3 = sides(pair, "y")
    v_far = shift(after(out_basis, z_1, z_3), "zlo", 1)
    in_z = everyone(after(in_rot, right_x), "zhi", 4)
    z_2 = jnp.concatenate(opposite(after(z_1, right_own), after(z_3, right_own), "zhi"), axis=-2)
    far = lax.all_gather(after(v_far, in_z, pair_1, pair_3), ("x", "core"), axis=0, tiled=False)

    in_1, in_3 = sides(in_z, "y")
    pair_2 = opposite(pair_1, pair_3, "y")
    in_2 = opposite(after(in_1, *pair_2), after(in_3, *pair_2), "y")
    far_1, far_3 = sides(z_2, "y")
    far_2 = opposite(far_1, far_3, "y")

    in_pieces = (in_z, in_1, *in_2, in_3)
    in_cut = in_2[0].shape[1]
    left_own = [in_z[:, SEQ_LEN:], in_1[:, SEQ_LEN:], in_3[:, SEQ_LEN:], in_2[1][:, SEQ_LEN - in_cut :]]
    left_other = shift(jnp.concatenate(left_own, axis=0), "core", 1)
    in_y = jnp.repeat(jnp.array((0, 1, 3, 2), jnp.int32), 4)
    columns = lax.rem(y - in_y + 4, 4) * 4 + lax.rem(block, 4)

    pieces = (own, own_1, *own_2, own_3, pair, pair_1, *pair_2, pair_3, z_2, far_1, *far_2, far_3)
    steps = [(k, z) for group in GROUPS for k in (0, 1, 3, 2) for z in group]
    y_steps, z_steps = (jnp.array(v, jnp.int32) for v in zip(*steps))
    numbers = lax.rem(y - y_steps + 4, 4) * 4 + lax.rem(zhi - z_steps + 4, 4)
    numbers = lax.rem(numbers - zlo * 8 + 16, 16).astype(jnp.int32)

    right_here = jnp.concatenate([right_own, shift(right_own, "core", 1)], axis=0)
    eig_t = jnp.transpose(eigenvalues)
    total = score(
        numbers, columns, lengths, pieces, in_pieces, near, far, right_here, eig_t, left_other
    )
    sums = jnp.sum(total, axis=1)
    sums = jnp.where(core == 0, sums, jnp.concatenate([sums[half:], sums[:half]]))
    queries = factors // RANK
    partial = jnp.sum(sums.reshape(queries, RANK), axis=1)
    pieces = lax.all_to_all(partial.reshape(feats, 1, 1), FEAT, 0, 0)
    return jnp.sum(pieces, axis=0)


def solution(mesh):
    fine = Mesh(mesh.devices.reshape(SIZES), AXES)
    in_specs = (
        P(TRAIN, FEAT),
        P(TRAIN, FEAT),
        P(TRAIN, FEAT),
        P(TRAIN, FEAT),
        P(None, FEAT),
        P(TRAIN, None),
        P(TRAIN, None),
        P(TRAIN),
    )
    return jax.shard_map(
        local, mesh=fine, in_specs=in_specs, out_specs=P(TRAIN, FEAT), check_vma=False
    )
```

```python
import functools

import jax
import jax.numpy as jnp
from jax import lax
from jax.experimental import pallas as pl
from jax.experimental.pallas import tpu as pltpu
from jax.sharding import Mesh, PartitionSpec as P

SEQ_LEN = 256
RANK = 8
VMEM_LIMIT = 16 << 20
SCORE_LIMIT = 54 << 20
GROUPS = ((0,), (1, 3), (2,))
PIECES = 20
damping = 0.01
AXES = ("zlo", "x", "core", "y", "zhi")
SIZES = (2, 4, 2, 4, 4)
TRAIN = ("zlo", "x", "core")
FEAT = ("y", "zhi")
over_rows = (((0,), (0,)), ((), ()))


def shift(block, axis, step):
    size = SIZES[AXES.index(axis)]
    return lax.ppermute(block, axis, [(i, (i + step) % size) for i in range(size)])


def sides(block, axis):
    return shift(block, axis, 1), shift(block, axis, -1)


def opposite(one, three, axis):
    cut = one.shape[-2] // 2
    return shift(one[..., :cut, :], axis, 1), shift(three[..., cut:, :], axis, -1)


def direct(block, axis):
    return [block] + [shift(block, axis, step) for step in (1, 2, 3)]


def after(value, *earlier):
    return lax.optimization_barrier((value, *earlier))[0]


def everyone(block, axes, size):
    return lax.all_to_all(jnp.broadcast_to(block[None], (size,) + block.shape), axes, 0, 0)


def rotate_in_kernel(order, lhs, rhs, out, acc, acc_left):
    step = pl.program_id(0)
    width = lhs.shape[2]
    half = acc_left.shape[0]

    @pl.when(step == 0)
    def _():
        acc[...] = jnp.zeros_like(acc)
        acc_left[...] = jnp.zeros_like(acc_left)

    basis = rhs[0, :, :width]
    acc[...] += jnp.dot(lhs[0], basis, preferred_element_type=jnp.float32)
    acc_left[...] += lax.dot_general(
        rhs[0, :, width:], basis, over_rows, preferred_element_type=jnp.float32
    )

    @pl.when(step == pl.num_programs(0) - 1)
    def _():
        rows = acc.shape[0]
        out[:rows] = acc[...].astype(out.dtype)
        core = order[pl.num_programs(0)]
        mine = jnp.where(core == 0, acc_left[:half // 2], acc_left[half // 2 :])
        out[rows:] = mine.astype(out.dtype)


def rotate_in(order, lhs, rhs):
    blocks, rows, depth = lhs.shape
    cols = depth
    factors = rhs.shape[2] - cols
    return pl.pallas_call(
        rotate_in_kernel,
        grid_spec=pltpu.PrefetchScalarGridSpec(
            num_scalar_prefetch=1,
            grid=(blocks,),
            in_specs=[
                pl.BlockSpec((1, rows, depth), lambda b, order: (b, 0, 0)),
                pl.BlockSpec((1, depth, cols + factors), lambda b, order: (order[b], 0, 0)),
            ],
            out_specs=pl.BlockSpec((rows + factors // 2, cols), lambda b, order: (0, 0)),
            scratch_shapes=[
                pltpu.VMEM((rows, cols), jnp.float32),
                pltpu.VMEM((factors, cols), jnp.float32),
            ],
        ),
        out_shape=jax.ShapeDtypeStruct((rows + factors // 2, cols), jnp.bfloat16),
        compiler_params=pltpu.CompilerParams(vmem_limit_bytes=VMEM_LIMIT),
    )(order, lhs, rhs)


def score_kernel(order, columns, live, *refs):
    lhs, rest = refs[:PIECES], refs[PIECES:]
    right, left, eig_hbm, near, far, out, met, rows, acc, eig, held, lhs_sems, eig_sems, sems = rest
    slots = held.shape[0]
    ahead, width = eig.shape[0], eig.shape[2]

    def bring(number):
        start = pl.multiple_of(columns[number] * width, width)
        return pltpu.make_async_copy(
            eig_hbm.at[:, pl.ds(start, width)], eig.at[number % ahead], eig_sems.at[number % ahead]
        )

    for number in range(ahead - 1):
        bring(number).start()
    half = near.shape[0]
    moves = {}
    for held_in, bases in ((met, ((0, 1), (5, 2), (10, 1))), (rows, ((15, 4),))):
        first = 0
        for base, count in bases:
            cut = lhs[base + 2].shape[1]
            for piece, row in ((base, 0), (base + 1, 0), (base + 4, 0), (base + 2, 0), (base + 3, cut)):
                target = held_in.at[pl.ds(first, count), pl.ds(row, lhs[piece].shape[1])]
                move = pltpu.make_async_copy(lhs[piece], target, lhs_sems.at[piece])
                moves.setdefault((held_in is met, first), []).append(move)
                move.start()
                if piece != base + 2:
                    first += count

    def fetch(number, act):
        slot = number % slots

        @pl.when(order[number] < half)
        def _():
            act(pltpu.make_async_copy(near.at[jnp.minimum(order[number], half - 1)], held.at[slot], sems.at[slot]))

        @pl.when(order[number] >= half)
        def _():
            act(pltpu.make_async_copy(far.at[jnp.maximum(order[number] - half, 0)], held.at[slot], sems.at[slot]))

    for number in range(slots - 1):
        fetch(number, lambda copy: copy.start())
    depth = near.shape[1]
    for number in range(met.shape[0]):
        if number + slots - 1 < met.shape[0]:
            fetch(number + slots - 1, lambda copy: copy.start())
        fetch(number, lambda copy: copy.wait())
        for move in moves.get((True, number), ()):
            move.wait()
        term = jnp.dot(
            met[number, :, :depth], held[number % slots], preferred_element_type=jnp.float32
        )
        if number == 0:
            acc[...] = term
        else:
            acc[...] += term
    position = lax.broadcasted_iota(jnp.int32, acc.shape, 0)
    out_t = jnp.where(position < live[0], acc[...], 0.0).astype(jnp.bfloat16).T
    seq = acc.shape[0]
    total = jnp.zeros(out.shape, jnp.float32)
    for i in range(rows.shape[0]):
        if i + ahead - 1 < rows.shape[0]:
            bring(i + ahead - 1).start()
        for move in moves.get((False, i), ()):
            move.wait()
        grad = jnp.dot(out_t, rows[i, :seq], preferred_element_type=jnp.float32)
        bring(i).wait()
        scaled = (grad / (eig[i % ahead] + damping)).astype(jnp.bfloat16)
        mapped = jnp.dot(right[...], scaled, preferred_element_type=jnp.float32)
        factors = jnp.concatenate([rows[i, seq:], left[i]], axis=0)
        total += mapped * factors.astype(jnp.float32)
    out[...] = total


def score(order, columns, live, lhs, rows, near, far, right, eig_t, left):
    (height, padded), cols = lhs[0].shape[1:], near.shape[2]
    factors, width = right.shape[0], rows[0].shape[2]
    vmem, smem = pl.BlockSpec(memory_space=pltpu.VMEM), pl.BlockSpec(memory_space=pltpu.SMEM)
    hbm = pl.BlockSpec(memory_space=pltpu.HBM)
    return pl.pallas_call(
        score_kernel,
        in_specs=[smem] * 3 + [hbm] * PIECES + [vmem] * 2 + [hbm] * 3,
        out_specs=vmem,
        scratch_shapes=[
            pltpu.VMEM((16, height, padded), jnp.bfloat16),
            pltpu.VMEM((16,) + rows[0].shape[1:], jnp.bfloat16),
            pltpu.VMEM((height, cols), jnp.float32),
            pltpu.VMEM((4, cols, width), jnp.float32),
            pltpu.VMEM((4,) + near.shape[1:], jnp.bfloat16),
            pltpu.SemaphoreType.DMA((PIECES,)),
            pltpu.SemaphoreType.DMA((4,)),
            pltpu.SemaphoreType.DMA((4,)),
        ],
        out_shape=jax.ShapeDtypeStruct((factors, width), jnp.float32),
        compiler_params=pltpu.CompilerParams(vmem_limit_bytes=SCORE_LIMIT),
    )(order, columns, live, *lhs, *rows, right, left, eig_t, near, far)


def local(
    activations, grad_outputs, in_basis, out_basis, eigenvalues, query_left, query_right, lengths
):
    zlo, x, core = lax.axis_index("zlo"), lax.axis_index("x"), lax.axis_index("core")
    y, zhi = lax.axis_index("y"), lax.axis_index("zhi")
    bf16, f32 = jnp.bfloat16, jnp.float32
    trains, feats = 16, 16
    factors = query_left.shape[1]
    share = factors // trains
    slab = out_basis.shape[1]
    width = in_basis.shape[1]

    u_own = jnp.concatenate([in_basis, query_left], axis=1)
    u_far = shift(u_own, "zlo", 1)
    u_all = lax.all_gather(jnp.stack([u_own, u_far]), ("x", "core"), axis=0, tiled=True)
    near = lax.all_gather(after(out_basis, u_far), ("x", "core"), axis=0, tiled=False)
    block = jnp.arange(feats, dtype=jnp.int32)
    u_place = lax.rem(block, 8) * 2 + lax.rem(zlo + block // 8, 2)

    right_part = lax.dot_general(query_right, out_basis, over_rows, preferred_element_type=f32)
    half = factors // 2
    low, high = right_part[:half], right_part[half:]
    right_core = jnp.where(core == 0, low, high) + shift(jnp.where(core == 0, high, low), "core", 1)
    right_pair = right_core + shift(right_core, "zlo", 1)
    right_x = right_pair + lax.ppermute(right_pair, "x", [(i, i ^ 1) for i in range(4)])

    act_z = everyone(after(activations, u_far), "zhi", 4)
    padding = -slab % 256
    own = jnp.pad(grad_outputs, ((0, 0), (0, padding)))[None]
    own_1, own_3 = sides(own, "y")

    act_all = everyone(after(act_z, own_1, own_3, right_core), "y", 4).reshape(feats, SEQ_LEN, width)
    z_1, z_3 = sides(after(own, act_z), "zhi")
    own_2 = opposite(own_1, own_3, "y")
    in_rot = rotate_in(
        jnp.concatenate([u_place, core[None].astype(jnp.int32)]),
        after(act_all, z_1, z_3, *own_2, right_pair),
        u_all,
    )

    pair = jnp.concatenate([z_1, z_3], axis=0)
    pair_1, pair_3 = sides(pair, "y")
    v_far = shift(after(out_basis, z_1, z_3), "zlo", 1)
    in_z = everyone(after(in_rot, right_x), "zhi", 4)
    z_2 = shift(after(own, in_rot), "zhi", 2)
    right_sum = right_x + lax.ppermute(after(right_x, in_rot), "x", [(i, i ^ 2) for i in range(4)])
    right_own = right_sum.astype(bf16)
    far = lax.all_gather(after(v_far, in_z, pair_1, pair_3, right_own), ("x", "core"), axis=0, tiled=False)

    in_1, in_3 = sides(in_z, "y")
    pair_2 = opposite(pair_1, pair_3, "y")
    in_2 = opposite(after(in_1, *pair_2), after(in_3, *pair_2), "y")
    far_1, far_3 = sides(after(z_2, in_1, in_3), "y")
    far_2 = opposite(far_1, far_3, "y")

    in_pieces = (in_z, in_1, *in_2, in_3)
    in_cut = in_2[0].shape[1]
    left_own = [in_z[:, SEQ_LEN:], in_1[:, SEQ_LEN:], in_3[:, SEQ_LEN:], in_2[1][:, SEQ_LEN - in_cut :]]
    left_other = shift(jnp.concatenate(left_own, axis=0), "core", 1)
    in_y = jnp.repeat(jnp.array((0, 1, 3, 2), jnp.int32), 4)
    columns = lax.rem(y - in_y + 4, 4) * 4 + lax.rem(block, 4)

    pieces = (own, own_1, *own_2, own_3, pair, pair_1, *pair_2, pair_3, z_2, far_1, *far_2, far_3)
    steps = [(k, z) for group in GROUPS for k in (0, 1, 3, 2) for z in group]
    y_steps, z_steps = (jnp.array(v, jnp.int32) for v in zip(*steps))
    numbers = lax.rem(y - y_steps + 4, 4) * 4 + lax.rem(zhi - z_steps + 4, 4)
    numbers = lax.rem(numbers - zlo * 8 + 16, 16).astype(jnp.int32)

    right_here = jnp.concatenate([right_own, shift(right_own, "core", 1)], axis=0)
    eig_t = jnp.transpose(eigenvalues)
    total = score(
        numbers, columns, lengths, pieces, in_pieces, near, far, right_here, eig_t, left_other
    )
    sums = jnp.sum(total, axis=1)
    sums = jnp.where(core == 0, sums, jnp.concatenate([sums[half:], sums[:half]]))
    queries = factors // RANK
    partial = jnp.sum(sums.reshape(queries, RANK), axis=1)
    pieces = lax.all_to_all(partial.reshape(feats, 1, 1), FEAT, 0, 0)
    return jnp.sum(pieces, axis=0)


def solution(mesh):
    fine = Mesh(mesh.devices.reshape(SIZES), AXES)
    in_specs = (
        P(TRAIN, FEAT),
        P(TRAIN, FEAT),
        P(TRAIN, FEAT),
        P(TRAIN, FEAT),
        P(None, FEAT),
        P(TRAIN, None),
        P(TRAIN, None),
        P(TRAIN),
    )
    return jax.shard_map(
        local, mesh=fine, in_specs=in_specs, out_specs=P(TRAIN, FEAT), check_vma=False
    )
```

```python
import functools

import jax
import jax.numpy as jnp
from jax import lax
from jax.experimental import pallas as pl
from jax.experimental.pallas import tpu as pltpu
from jax.sharding import Mesh, PartitionSpec as P

SEQ_LEN = 256
RANK = 8
VMEM_LIMIT = 16 << 20
SCORE_LIMIT = 54 << 20
GROUPS = ((0,), (1, 3), (2,))
PIECES = 20
damping = 0.01
AXES = ("zlo", "x", "core", "y", "zhi")
SIZES = (2, 4, 2, 4, 4)
TRAIN = ("zlo", "x", "core")
FEAT = ("y", "zhi")
over_rows = (((0,), (0,)), ((), ()))


def shift(block, axis, step):
    size = SIZES[AXES.index(axis)]
    return lax.ppermute(block, axis, [(i, (i + step) % size) for i in range(size)])


def sides(block, axis):
    return shift(block, axis, 1), shift(block, axis, -1)


def opposite(one, three, axis):
    cut = one.shape[-2] // 2
    return shift(one[..., :cut, :], axis, 1), shift(three[..., cut:, :], axis, -1)


def direct(block, axis):
    return [block] + [shift(block, axis, step) for step in (1, 2, 3)]


def after(value, *earlier):
    return lax.optimization_barrier((value, *earlier))[0]


def everyone(block, axes, size):
    return lax.all_to_all(jnp.broadcast_to(block[None], (size,) + block.shape), axes, 0, 0)


def rotate_in_kernel(order, lhs, rhs, out, acc, acc_left):
    step = pl.program_id(0)
    width = lhs.shape[2]
    half = acc_left.shape[0]

    @pl.when(step == 0)
    def _():
        acc[...] = jnp.zeros_like(acc)
        acc_left[...] = jnp.zeros_like(acc_left)

    basis = rhs[0, :, :width]
    acc[...] += jnp.dot(lhs[0], basis, preferred_element_type=jnp.float32)
    acc_left[...] += lax.dot_general(
        rhs[0, :, width:], basis, over_rows, preferred_element_type=jnp.float32
    )

    @pl.when(step == pl.num_programs(0) - 1)
    def _():
        rows = acc.shape[0]
        out[:rows] = acc[...].astype(out.dtype)
        core = order[pl.num_programs(0)]
        mine = jnp.where(core == 0, acc_left[:half // 2], acc_left[half // 2 :])
        out[rows:] = mine.astype(out.dtype)


def rotate_in(order, lhs, rhs):
    blocks, rows, depth = lhs.shape
    cols = depth
    factors = rhs.shape[2] - cols
    return pl.pallas_call(
        rotate_in_kernel,
        grid_spec=pltpu.PrefetchScalarGridSpec(
            num_scalar_prefetch=1,
            grid=(blocks,),
            in_specs=[
                pl.BlockSpec((1, rows, depth), lambda b, order: (b, 0, 0)),
                pl.BlockSpec((1, depth, cols + factors), lambda b, order: (order[b], 0, 0)),
            ],
            out_specs=pl.BlockSpec((rows + factors // 2, cols), lambda b, order: (0, 0)),
            scratch_shapes=[
                pltpu.VMEM((rows, cols), jnp.float32),
                pltpu.VMEM((factors, cols), jnp.float32),
            ],
        ),
        out_shape=jax.ShapeDtypeStruct((rows + factors // 2, cols), jnp.bfloat16),
        compiler_params=pltpu.CompilerParams(vmem_limit_bytes=VMEM_LIMIT),
    )(order, lhs, rhs)


def score_kernel(order, columns, live, *refs):
    lhs, rest = refs[:PIECES], refs[PIECES:]
    right, left, eig_hbm, near, far, out, met, rows, acc, eig, held, lhs_sems, eig_sems, sems = rest
    slots = held.shape[0]
    ahead, width = eig.shape[0], eig.shape[2]

    def bring(number):
        start = pl.multiple_of(columns[number] * width, width)
        return pltpu.make_async_copy(
            eig_hbm.at[:, pl.ds(start, width)], eig.at[number % ahead], eig_sems.at[number % ahead]
        )

    for number in range(ahead - 1):
        bring(number).start()
    half = near.shape[0]
    moves = {}
    for held_in, bases in ((met, ((0, 1), (5, 2), (10, 1))), (rows, ((15, 4),))):
        first = 0
        for base, count in bases:
            cut = lhs[base + 2].shape[1]
            for piece, row in ((base, 0), (base + 1, 0), (base + 4, 0), (base + 2, 0), (base + 3, cut)):
                target = held_in.at[pl.ds(first, count), pl.ds(row, lhs[piece].shape[1])]
                move = pltpu.make_async_copy(lhs[piece], target, lhs_sems.at[piece])
                moves.setdefault((held_in is met, first), []).append(move)
                move.start()
                if piece != base + 2:
                    first += count

    def fetch(number, act):
        slot = number % slots

        @pl.when(order[number] < half)
        def _():
            act(pltpu.make_async_copy(near.at[jnp.minimum(order[number], half - 1)], held.at[slot], sems.at[slot]))

        @pl.when(order[number] >= half)
        def _():
            act(pltpu.make_async_copy(far.at[jnp.maximum(order[number] - half, 0)], held.at[slot], sems.at[slot]))

    for number in range(slots - 1):
        fetch(number, lambda copy: copy.start())
    depth = near.shape[1]
    for number in range(met.shape[0]):
        if number + slots - 1 < met.shape[0]:
            fetch(number + slots - 1, lambda copy: copy.start())
        fetch(number, lambda copy: copy.wait())
        for move in moves.get((True, number), ()):
            move.wait()
        term = jnp.dot(
            met[number, :, :depth], held[number % slots], preferred_element_type=jnp.float32
        )
        if number == 0:
            acc[...] = term
        else:
            acc[...] += term
    position = lax.broadcasted_iota(jnp.int32, acc.shape, 0)
    out_t = jnp.where(position < live[0], acc[...], 0.0).astype(jnp.bfloat16).T
    seq = acc.shape[0]
    total = jnp.zeros(out.shape, jnp.float32)
    for i in range(rows.shape[0]):
        if i + ahead - 1 < rows.shape[0]:
            bring(i + ahead - 1).start()
        for move in moves.get((False, i), ()):
            move.wait()
        grad = jnp.dot(out_t, rows[i, :seq], preferred_element_type=jnp.float32)
        bring(i).wait()
        scaled = (grad / (eig[i % ahead] + damping)).astype(jnp.bfloat16)
        mapped = jnp.dot(right[...], scaled, preferred_element_type=jnp.float32)
        factors = jnp.concatenate([rows[i, seq:], left[i]], axis=0)
        total += mapped * factors.astype(jnp.float32)
    out[...] = total


def score(order, columns, live, lhs, rows, near, far, right, eig_t, left):
    (height, padded), cols = lhs[0].shape[1:], near.shape[2]
    factors, width = right.shape[0], rows[0].shape[2]
    vmem, smem = pl.BlockSpec(memory_space=pltpu.VMEM), pl.BlockSpec(memory_space=pltpu.SMEM)
    hbm = pl.BlockSpec(memory_space=pltpu.HBM)
    return pl.pallas_call(
        score_kernel,
        in_specs=[smem] * 3 + [hbm] * PIECES + [vmem] * 2 + [hbm] * 3,
        out_specs=vmem,
        scratch_shapes=[
            pltpu.VMEM((16, height, padded), jnp.bfloat16),
            pltpu.VMEM((16,) + rows[0].shape[1:], jnp.bfloat16),
            pltpu.VMEM((height, cols), jnp.float32),
            pltpu.VMEM((8, cols, width), jnp.float32),
            pltpu.VMEM((8,) + near.shape[1:], jnp.bfloat16),
            pltpu.SemaphoreType.DMA((PIECES,)),
            pltpu.SemaphoreType.DMA((8,)),
            pltpu.SemaphoreType.DMA((8,)),
        ],
        out_shape=jax.ShapeDtypeStruct((factors, width), jnp.float32),
        compiler_params=pltpu.CompilerParams(vmem_limit_bytes=SCORE_LIMIT),
    )(order, columns, live, *lhs, *rows, right, left, eig_t, near, far)


def local(
    activations, grad_outputs, in_basis, out_basis, eigenvalues, query_left, query_right, lengths
):
    zlo, x, core = lax.axis_index("zlo"), lax.axis_index("x"), lax.axis_index("core")
    y, zhi = lax.axis_index("y"), lax.axis_index("zhi")
    bf16, f32 = jnp.bfloat16, jnp.float32
    trains, feats = 16, 16
    factors = query_left.shape[1]
    share = factors // trains
    slab = out_basis.shape[1]
    width = in_basis.shape[1]

    u_own = jnp.concatenate([in_basis, query_left], axis=1)
    u_far = shift(u_own, "zlo", 1)
    u_all = lax.all_gather(jnp.stack([u_own, u_far]), ("x", "core"), axis=0, tiled=True)
    near = lax.all_gather(after(out_basis, u_far), ("x", "core"), axis=0, tiled=False)
    block = jnp.arange(feats, dtype=jnp.int32)
    u_place = lax.rem(block, 8) * 2 + lax.rem(zlo + block // 8, 2)

    right_part = lax.dot_general(query_right, out_basis, over_rows, preferred_element_type=f32)
    half = factors // 2
    low, high = right_part[:half], right_part[half:]
    right_core = jnp.where(core == 0, low, high) + shift(jnp.where(core == 0, high, low), "core", 1)
    right_pair = right_core + shift(right_core, "zlo", 1)
    right_x = right_pair + lax.ppermute(right_pair, "x", [(i, i ^ 1) for i in range(4)])

    act_z = everyone(after(activations, u_far), "zhi", 4)
    padding = -slab % 256
    own = jnp.pad(grad_outputs, ((0, 0), (0, padding)))[None]
    own_1, own_3 = sides(own, "y")

    act_all = everyone(after(act_z, own_1, own_3, right_core), "y", 4).reshape(feats, SEQ_LEN, width)
    z_1, z_3 = sides(after(own, act_z), "zhi")
    own_2 = opposite(own_1, own_3, "y")
    in_rot = rotate_in(
        jnp.concatenate([u_place, core[None].astype(jnp.int32)]),
        after(act_all, z_1, z_3, *own_2, right_pair),
        u_all,
    )

    pair = jnp.concatenate([z_1, z_3], axis=0)
    pair_1, pair_3 = sides(pair, "y")
    v_far = shift(after(out_basis, z_1, z_3), "zlo", 1)
    in_z = everyone(after(in_rot, right_x), "zhi", 4)
    z_2 = shift(after(own, in_rot), "zhi", 2)
    right_sum = right_x + lax.ppermute(after(right_x, in_rot), "x", [(i, i ^ 2) for i in range(4)])
    right_own = right_sum.astype(bf16)
    far = lax.all_gather(after(v_far, in_z, pair_1, pair_3, right_own), ("x", "core"), axis=0, tiled=False)

    in_1, in_3 = sides(in_z, "y")
    pair_2 = opposite(pair_1, pair_3, "y")
    in_2 = opposite(after(in_1, *pair_2), after(in_3, *pair_2), "y")
    far_1, far_3 = sides(after(z_2, in_1, in_3), "y")
    far_2 = opposite(far_1, far_3, "y")

    in_pieces = (in_z, in_1, *in_2, in_3)
    in_cut = in_2[0].shape[1]
    left_own = [in_z[:, SEQ_LEN:], in_1[:, SEQ_LEN:], in_3[:, SEQ_LEN:], in_2[1][:, SEQ_LEN - in_cut :]]
    left_other = shift(jnp.concatenate(left_own, axis=0), "core", 1)
    in_y = jnp.repeat(jnp.array((0, 1, 3, 2), jnp.int32), 4)
    columns = lax.rem(y - in_y + 4, 4) * 4 + lax.rem(block, 4)

    pieces = (own, own_1, *own_2, own_3, pair, pair_1, *pair_2, pair_3, z_2, far_1, *far_2, far_3)
    steps = [(k, z) for group in GROUPS for k in (0, 1, 3, 2) for z in group]
    y_steps, z_steps = (jnp.array(v, jnp.int32) for v in zip(*steps))
    numbers = lax.rem(y - y_steps + 4, 4) * 4 + lax.rem(zhi - z_steps + 4, 4)
    numbers = lax.rem(numbers - zlo * 8 + 16, 16).astype(jnp.int32)

    right_here = jnp.concatenate([right_own, shift(right_own, "core", 1)], axis=0)
    eig_t = jnp.transpose(eigenvalues)
    total = score(
        numbers, columns, lengths, pieces, in_pieces, near, far, right_here, eig_t, left_other
    )
    sums = jnp.sum(total, axis=1)
    sums = jnp.where(core == 0, sums, jnp.concatenate([sums[half:], sums[:half]]))
    queries = factors // RANK
    partial = jnp.sum(sums.reshape(queries, RANK), axis=1)
    pieces = lax.all_to_all(partial.reshape(feats, 1, 1), FEAT, 0, 0)
    return jnp.sum(pieces, axis=0)


def solution(mesh):
    fine = Mesh(mesh.devices.reshape(SIZES), AXES)
    in_specs = (
        P(TRAIN, FEAT),
        P(TRAIN, FEAT),
        P(TRAIN, FEAT),
        P(TRAIN, FEAT),
        P(None, FEAT),
        P(TRAIN, None),
        P(TRAIN, None),
        P(TRAIN),
    )
    return jax.shard_map(
        local, mesh=fine, in_specs=in_specs, out_specs=P(TRAIN, FEAT), check_vma=False
    )
```
